256 devices in a mesh: section: 16 (over x, z_lo), expert: 16 (over y, z_hi, core).
Axes of the slice: x: 4, y: 4, z: 8 (z_hi: 2, z_lo: 4; z = z_hi * 4 + z_lo), core: 2. Of those that a mesh axis runs over, the one named last changes fastest.
Arguments:
- fwd_tokens: bfloat16 [16, 2048, 2048], P('section', 'expert'), may hold values from -6 to 6
- fwd_experts: int32 [16, 2048, 8], P('section', 'expert'), may hold values from 0 to 15, all different within a row; in each aligned block of 128 rows (0 to 127, 128 to 255, ..., all dimensions but the last counted through in order) at most 80 rows name the same one
- fwd_gates: float32 [16, 2048, 8], P('section', 'expert'), may hold values from 0.1 to 0.5
- gate_proj: bfloat16 [16, 16, 2048, 384], P('section', 'expert'), may hold values from -0.125 to 0.125
- up_proj: bfloat16 [16, 16, 2048, 384], P('section', 'expert'), may hold values from -0.125 to 0.125
- down_proj: bfloat16 [16, 16, 384, 2048], P('section', 'expert'), may hold values from -0.3125 to 0.3125
- bwd_grads: bfloat16 [16, 2048, 2048], P('section', 'expert'), may hold values from -6 to 6
- bwd_experts: int32 [16, 2048, 8], P('section', 'expert'), may hold values from 0 to 15, all different within a row; in each aligned block of 128 rows (0 to 127, 128 to 255, ..., all dimensions but the last counted through in order) at most 80 rows name the same one
- bwd_gates: float32 [16, 2048, 8], P('section', 'expert'), may hold values from 0.1 to 0.5
- saved_pre: bfloat16 [16, 16, 16, 80, 768], P('section', None, 'expert'), may hold values from -6 to 6
Outputs:
- fwd_next: bfloat16 [16, 2048, 2048], P('section', 'expert')
- grad_prev: bfloat16 [16, 2048, 2048], P('section', 'expert')
The draws below stay inside these ranges and needn't reach their ends.
Inputs may be any that keep to these rules, and one draw needn't show every extreme that they name: `fwd_experts`: each token names 8 different experts; within a section, the 128 tokens of one index of expert name no expert more than 80 times, a bound that some block reaches. `bwd_experts`: as for fwd_experts.
All inputs are finite; a program needn't handle non-finite values.
Results may differ from the reference program's by a relative error of at most 0.0053.
Values may be sent and summed in bfloat16 or wider, within the bound.
A program may use at most 128 MiB of HBM per device.

```python
import math
import jax
import jax.numpy as jnp
import numpy as np
from jax import lax

D = 2048
FF = 384
TOP = 8
TOK_DEV = 128
EXPERTS = 16
CAP = 80
TOKENS = 2048
N_SECTION = 16
N_EXPERT = 16


def block_scale(own_key, extent, split, low, largest):
    level = 1.0
    for dim, shards_of in split:
        steps = jax.random.uniform(jax.random.fold_in(jax.random.fold_in(own_key, 6), dim), (shards_of,), jnp.float32, low / len(split), largest / len(split))
        level = level * jnp.repeat(jnp.exp(steps), extent[dim] // shards_of).reshape((-1,) + (1,) * (len(extent) - 1 - dim))
    return level


def shared_out(key, own, number, rows, number_of, top, bound, skew):
    sequence = jax.random.permutation(key, number_of)
    packed, usual = portions_of(number_of, rows * top, bound, skew, True), portions_of(number_of, rows * top, bound, skew, False)
    places = jnp.arange(number_of)

    def named(lengths, rotation):
        used = int((lengths > 0).sum())
        fixed = max(1, used // 4)
        passed = fixed + (places - fixed + rotation * (used - fixed)) % max(1, number_of - fixed)
        return jnp.zeros((number_of,), jnp.int32).at[sequence[jnp.where(places < fixed, places, passed)]].set(jnp.asarray(lengths, jnp.int32))

    lengths = jnp.where(number % 4 == 0, named(packed, number // 4), named(usual, number - number // 4 - 1))
    mixed = jax.random.permutation(jax.random.fold_in(own, 3), number_of)
    source_of, receiver = mixed[0:number_of // 2 * 2:2], mixed[1:number_of // 2 * 2:2]
    margin = jnp.minimum(lengths[source_of] - 1, bound - lengths[receiver]) // 2
    margin = jnp.where((source_of == sequence[0]) | (receiver == sequence[0]) | (lengths[receiver] == 0), 0, jnp.maximum(margin, 0))
    passed = jax.random.randint(jax.random.fold_in(own, 4), (number_of // 2,), 0, 1 << 20) % (margin + 1)
    lengths = lengths.at[source_of].add(-passed).at[receiver].add(passed)
    members = jnp.searchsorted(jnp.cumsum(lengths), jnp.arange(rows * top), side="right").astype(jnp.int32)
    grid = members.reshape(top, rows).T
    grid = grid[jax.random.permutation(jax.random.fold_in(own, 1), rows)]
    rotation = jax.random.randint(jax.random.fold_in(own, 2), (rows, 1), 0, top)
    return jnp.take_along_axis(grid, (jnp.arange(top)[None, :] + rotation) % top, axis=1)


def portions_of(count, total, limit, slope, full):
    weights = [(1 << 20) // math.isqrt(rank ** slope) + 1 for rank in range(1, count + 1)]
    largest = limit if full else min(limit, max(-(-total // count), total * weights[0] // sum(weights)))
    least = 1 if total - largest >= count - 1 else 0
    holding, spare = [largest] + [least] * (count - 1), total - largest - least * (count - 1)
    while spare > 0:
        free = [i for i in range(1, count) if holding[i] < largest] or [i for i in range(1, count) if holding[i] < limit]
        mass, remaining = sum([weights[i] for i in free]), spare
        for i in free:
            extra = min(limit - holding[i], max(1, remaining * weights[i] // mass), spare)
            holding[i] = holding[i] + extra
            spare = spare - extra
    return np.array(holding)


def bell_draw(own_key, dims, scale, limit, shards=(), held_as=jnp.bfloat16):
    values = scale * jax.random.normal(own_key, dims, jnp.float32)
    if shards:
        values = values * block_scale(own_key, dims, shards, -0.22, 0.18)
    return jnp.clip(values, -limit, limit).astype(held_as)


def setup_inputs(seed: int = 0) -> dict:
    seeds = jax.random.split(jax.random.key(seed), 11)
    fwd_tokens = bell_draw(seeds[0], (N_SECTION, TOKENS, D), 1.0, 6.0, ((0, 16), (1, 16)))
    fwd_experts_keys = jax.random.split(jax.random.fold_in(seeds[1], 1), N_SECTION * TOKENS // TOK_DEV)
    fwd_experts_turns = jax.random.permutation(jax.random.fold_in(seeds[1], 3), N_SECTION * TOKENS // TOK_DEV)
    fwd_experts = jax.vmap(lambda own, number: shared_out(jax.random.fold_in(seeds[1], 2), own, number, TOK_DEV, EXPERTS, TOP, CAP, 2))(fwd_experts_keys, fwd_experts_turns).reshape((N_SECTION, TOKENS, TOP))
    fwd_gates = jnp.clip(jnp.exp(math.log(0.5) - 1.609438 * jax.random.uniform(seeds[2], (N_SECTION, TOKENS, TOP), jnp.float32) ** block_scale(seeds[2], (N_SECTION, TOKENS, TOP), ((0, 16), (1, 16)), -0.2, 0.2)), 0.1, 0.5)
    gate_proj = bell_draw(seeds[3], (N_SECTION, EXPERTS, D, FF), D ** -0.5, 0.125, ((0, 16), (1, 16)))
    up_proj = bell_draw(seeds[4], (N_SECTION, EXPERTS, D, FF), D ** -0.5, 0.125, ((0, 16), (1, 16)))
    down_proj = bell_draw(seeds[5], (N_SECTION, EXPERTS, FF, D), FF ** -0.5, 0.3125, ((0, 16), (1, 16)))
    bwd_grads = bell_draw(seeds[6], (N_SECTION, TOKENS, D), 1.0, 6.0, ((0, 16), (1, 16)))
    bwd_experts_keys = jax.random.split(jax.random.fold_in(seeds[7], 1), N_SECTION * TOKENS // TOK_DEV)
    bwd_experts_turns = jax.random.permutation(jax.random.fold_in(seeds[7], 3), N_SECTION * TOKENS // TOK_DEV)
    bwd_experts = jax.vmap(lambda own, number: shared_out(jax.random.fold_in(seeds[7], 2), own, number, TOK_DEV, EXPERTS, TOP, CAP, 2))(bwd_experts_keys, bwd_experts_turns).reshape((N_SECTION, TOKENS, TOP))
    bwd_gates = jnp.clip(jnp.exp(math.log(0.5) - 1.609438 * jax.random.uniform(seeds[8], (N_SECTION, TOKENS, TOP), jnp.float32) ** block_scale(seeds[8], (N_SECTION, TOKENS, TOP), ((0, 16), (1, 16)), -0.2, 0.2)), 0.1, 0.5)
    saved_pre = bell_draw(seeds[9], (N_SECTION, N_EXPERT, EXPERTS, CAP, 2 * FF), 1.0, 6.0, ((0, 16), (2, 16)))
    return dict(fwd_tokens=fwd_tokens, fwd_experts=fwd_experts, fwd_gates=fwd_gates, gate_proj=gate_proj, up_proj=up_proj, down_proj=down_proj, bwd_grads=bwd_grads, bwd_experts=bwd_experts, bwd_gates=bwd_gates, saved_pre=saved_pre)


def slot_index(expert_ids):
    onehot = jnp.sum((expert_ids[:, :, None] == jnp.arange(EXPERTS, dtype=jnp.int32)[None, None, :]).astype(jnp.int32), axis=1)
    blocked = onehot.reshape(N_EXPERT, TOK_DEV, EXPERTS)
    ahead = (jnp.cumsum(blocked, axis=1) - blocked).astype(jnp.int32).reshape(N_EXPERT * TOK_DEV, EXPERTS)
    place = jnp.take_along_axis(ahead, expert_ids, axis=1).astype(jnp.int32)
    source = (jnp.arange(N_EXPERT * TOK_DEV, dtype=jnp.int32) // TOK_DEV)[:, None]
    return ((source * EXPERTS + expert_ids) * CAP + place).astype(jnp.int32)


def scatter_pairs(pair_values, slot_rows):
    buffer = jnp.zeros((N_EXPERT * EXPERTS * CAP, D), pair_values.dtype)
    buffer = buffer.at[slot_rows.reshape(-1)].set(pair_values)
    return buffer.reshape(N_EXPERT, EXPERTS, CAP, D)


def section_window(operands):
    (fwd_tokens, fwd_experts, fwd_gates, gate_proj, up_proj, down_proj,
     bwd_grads, bwd_experts, bwd_gates, saved_pre) = operands
    gate_f = gate_proj.astype(jnp.float32)
    up_f = up_proj.astype(jnp.float32)
    down_f = down_proj.astype(jnp.float32)

    fwd_slot = slot_index(fwd_experts)
    dispatched = scatter_pairs(jnp.repeat(fwd_tokens, TOP, axis=0), fwd_slot).astype(jnp.float32)
    gate_act = jnp.einsum("necd,edf->necf", dispatched, gate_f)
    up_act = jnp.einsum("necd,edf->necf", dispatched, up_f)
    hidden = (jax.nn.silu(gate_act) * up_act).astype(jnp.bfloat16)
    expert_out = jnp.einsum("necf,efd->necd", hidden.astype(jnp.float32), down_f).astype(jnp.bfloat16)
    picked = expert_out.reshape(-1, D)[fwd_slot].astype(jnp.float32)
    mixed = (fwd_tokens.astype(jnp.float32) + jnp.sum(fwd_gates[:, :, None] * picked, axis=1)).astype(jnp.bfloat16)

    bwd_slot = slot_index(bwd_experts)
    scaled_grad = (bwd_gates[:, :, None] * bwd_grads.astype(jnp.float32)[:, None, :]).astype(jnp.bfloat16)
    grad_dispatched = scatter_pairs(scaled_grad.reshape(-1, D), bwd_slot).astype(jnp.float32)
    saved_f = saved_pre.astype(jnp.float32)
    pre_gate = saved_f[..., :FF]
    pre_up = saved_f[..., FF:]
    grad_hidden = jnp.einsum("necd,efd->necf", grad_dispatched, down_f)
    sigma = jax.nn.sigmoid(pre_gate)
    grad_gate = (grad_hidden * pre_up * sigma * (1.0 + pre_gate * (1.0 - sigma))).astype(jnp.bfloat16)
    grad_up = (grad_hidden * pre_gate * sigma).astype(jnp.bfloat16)
    grad_slot = jnp.einsum("necf,edf->necd", grad_gate.astype(jnp.float32), gate_f)
    grad_slot = (grad_slot + jnp.einsum("necf,edf->necd", grad_up.astype(jnp.float32), up_f)).astype(jnp.bfloat16)
    gathered = grad_slot.reshape(-1, D)[bwd_slot].astype(jnp.float32)
    grad_tokens = (bwd_grads.astype(jnp.float32) + jnp.sum(gathered, axis=1)).astype(jnp.bfloat16)
    return mixed, grad_tokens


def reference(fwd_tokens, fwd_experts, fwd_gates, gate_proj, up_proj, down_proj,
              bwd_grads, bwd_experts, bwd_gates, saved_pre):
    mixed, grad_tokens = lax.map(section_window, (fwd_tokens, fwd_experts, fwd_gates, gate_proj, up_proj, down_proj,
                                                bwd_grads, bwd_experts, bwd_gates, saved_pre))
    fwd_next = jnp.roll(mixed, 1, axis=0)
    grad_prev = jnp.roll(grad_tokens, -1, axis=0)
    return fwd_next, grad_prev
```

```python
import jax
import jax.numpy as jnp
from jax import lax
from jax.experimental import pallas as pl
from jax.experimental.pallas import tpu as pltpu
from jax.sharding import PartitionSpec as P

Y_SIZE, HALVES, CORES = 4, 2, 2
PIECE = 32
MESH = pl.DeviceIdType.MESH
F32, BF16 = jnp.float32, jnp.bfloat16


def dot(a, b):
    return lax.dot_general(a, b, (((1,), (0,)), ((), ())), preferred_element_type=F32)


def dot_t(a, b):
    return lax.dot_general(a, b, (((1,), (1,)), ((), ())), preferred_element_type=F32)


def body(
    tab_in, xf, xb, wg, wu, wd, saved, out_f, out_b,
    tok, tab, wgu, wdn, sav, xs, ys, act, hid, sel, sel_t, sgate, chosen, part, opp, near, rel,
    dma_send, dma_recv, dma_local,
):
    section, expert = lax.axis_index("section"), lax.axis_index("expert")
    sections = lax.axis_size("section")
    y, h, c = expert // (HALVES * CORES), (expert // CORES) % HALVES, expert % CORES
    rows, width = xf.shape
    units = wg.shape[1]
    cap = saved.shape[1]
    half = rows // 2
    lanes = 512

    def at(dy, dh=0, dc=0, ds=0):
        return (
            (section + ds + sections) % sections,
            (((y + dy + Y_SIZE) % Y_SIZE) * HALVES + (h + dh) % HALVES) * CORES + (c + dc) % CORES,
        )

    up, down, across, twin = at(1), at(-1), at(0, 1), at(0, 0, 1)
    nexts = (at(0, 0, 0, 1), at(0, 1, 0, 1))
    prevs = (at(0, 0, 0, -1), at(0, 1, 0, -1))

    count = [0, 0]
    remote = []

    def send(src, dst, device):
        i = count[0]
        count[0] += 1
        copy = pltpu.make_async_remote_copy(
            src_ref=src, dst_ref=dst, send_sem=dma_send.at[i], recv_sem=dma_recv.at[i],
            device_id=device, device_id_type=MESH,
        )
        remote.append(copy)
        return copy

    def local(src, dst):
        i = count[1]
        count[1] += 1
        return pltpu.make_async_copy(src, dst, dma_local.at[i])

    barrier = pltpu.get_barrier_semaphore()
    greeted = (up, down, across, twin) + nexts + prevs
    for device in greeted:
        pl.semaphore_signal(barrier, inc=1, device_id=device, device_id_type=MESH)

    inputs = (xf, xb)
    load_tok = [local(inputs[d], tok.at[d, 0]) for d in range(2)]
    load_w = [
        local(wg, wgu.at[0, :, pl.ds(0, units)]),
        local(wu, wgu.at[0, :, pl.ds(units, units)]),
        local(wd, wdn.at[0]),
    ]

    def block_of(j, core):
        hh, dy = j // Y_SIZE, j % Y_SIZE
        return (((y + dy) % Y_SIZE) * HALVES + (h + hh) % HALVES) * CORES + core

    load_s = [local(saved.at[block_of(j, c)], sav.at[0, j]) for j in range(8)]
    for copy in load_tok + load_w + load_s:
        copy.start()
    tab[0] = tab_in[...]
    pl.semaphore_wait(barrier, len(greeted))

    low, high = pl.ds(0, half), pl.ds(half, half)
    tab_z = send(tab.at[0], tab.at[4], across)
    tab_y = [(send(tab.at[4 * g], tab.at[4 * g + 3], up), send(tab.at[4 * g], tab.at[4 * g + 1], down)) for g in range(2)]
    tab_o = [send(tab.at[4 * g + 3], tab.at[4 * g + 2], up) for g in range(2)]

    def source(d, g, part_rows):
        return inputs[d].at[part_rows] if g == 0 else tok.at[d, 4, part_rows]

    own = {}
    fwd = {}
    over = {}
    for d in range(2):
        for i, r in enumerate((low, high)):
            over[d, i] = send(inputs[d].at[r], tok.at[d, 4, r], across)
        for g in range(2):
            for i, r in enumerate((low, high)):
                own[d, g, 0, i] = send(source(d, g, r), tok.at[d, 4 * g + 3, r], up)
                own[d, g, 1, i] = send(source(d, g, r), tok.at[d, 4 * g + 1, r], down)
            fwd[d, g, 0] = send(tok.at[d, 4 * g + 3, low], tok.at[d, 4 * g + 2, low], up)
            fwd[d, g, 1] = send(tok.at[d, 4 * g + 1, high], tok.at[d, 4 * g + 2, high], down)
    twin_w = [
        send(wg, wgu.at[1, :, pl.ds(0, units)], twin),
        send(wu, wgu.at[1, :, pl.ds(units, units)], twin),
        send(wd, wdn.at[1], twin),
    ]
    twin_s = [send(saved.at[block_of(j, 1 - c)], sav.at[1, j], twin) for j in range(8)]

    def start_own(d, g, i):
        own[d, g, 0, i].start()
        own[d, g, 1, i].start()

    def forward(d, g):
        own[d, g, 0, 0].wait_recv()
        fwd[d, g, 0].start()
        own[d, g, 1, 1].wait_recv()
        fwd[d, g, 1].start()

    def complete(d, g):
        own[d, g, 0, 1].wait_recv()
        own[d, g, 1, 0].wait_recv()
        fwd[d, g, 0].wait_recv()
        fwd[d, g, 1].wait_recv()

    experts = [(y * HALVES + h) * CORES + c, (y * HALVES + h) * CORES + (1 - c)]

    def select(d, g):
        for j in range(4):
            names = tab[4 * g + j, 16 * d : 16 * d + 8, :]
            gates = tab[4 * g + j, 16 * d + 8 : 16 * d + 16, :]
            for m in range(2):
                hit = names == experts[m].astype(F32)
                chosen[2 * j + m : 2 * j + m + 1, :] = jnp.sum(jnp.where(hit, 1.0, 0.0), axis=0, keepdims=True)
                chosen[8 + 2 * j + m : 9 + 2 * j + m, :] = jnp.sum(jnp.where(hit, gates, 0.0), axis=0, keepdims=True)
        earlier = lax.broadcasted_iota(jnp.int32, (rows, rows), 0) < lax.broadcasted_iota(jnp.int32, (rows, rows), 1)
        ahead = dot(chosen[0:8, :].astype(BF16), jnp.where(earlier, 1.0, 0.0).astype(BF16))
        place = lax.broadcasted_iota(jnp.int32, (cap, rows), 0).astype(F32)
        for j in range(4):
            for m in range(2):
                i = 2 * j + m
                taken = (place == ahead[i : i + 1, :]) & (chosen[i : i + 1, :] > 0.5)
                one = jnp.where(taken, 1.0, 0.0)
                sel[j, m * cap : (m + 1) * cap, :] = one
                sgate[j, m] = jnp.sum(one * chosen[8 + i : 9 + i, :], axis=1, keepdims=True)
            sel_t[j] = jnp.transpose(sel[j]).astype(BF16)

    def dispatch(d, g):
        for j in range(4):
            one = sel[j].astype(BF16)

            @pl.loop(0, width // lanes)
            def _(n):
                at_n = pl.ds(pl.multiple_of(n * lanes, lanes), lanes)
                moved = dot(one, tok[d, 4 * g + j, :, at_n]).reshape(2, cap, lanes)
                if d == 1:
                    moved = moved * sgate[j]
                xs[j, :, :, at_n] = moved.astype(BF16)

    def collect(d, g):
        for j in range(4):
            one = sel_t[j]

            @pl.loop(0, width // lanes)
            def _(n):
                at_n = pl.ds(pl.multiple_of(n * lanes, lanes), lanes)
                summed = dot(one, ys[j, :, :, at_n].reshape(2 * cap, lanes))
                part[d, 4 * g + j, :, at_n] = summed.astype(BF16)

    def compute_f(g):
        select(0, g)
        dispatch(0, g)
        for m in range(2):
            @pl.loop(0, 2 * units // 256)
            def _(n):
                at_n = pl.ds(pl.multiple_of(n * 256, 256), 256)
                act[:, at_n] = dot(xs[:, m].reshape(4 * cap, width), wgu[m, :, at_n])

            gate = act[:, 0:units]
            hid[:, 0:units] = (gate / (1.0 + jnp.exp(-gate)) * act[:, units : 2 * units]).astype(BF16)

            @pl.loop(0, width // lanes)
            def _(n):
                at_n = pl.ds(pl.multiple_of(n * lanes, lanes), lanes)
                made = dot(hid[:, 0:units], wdn[m, :, at_n]).reshape(4, cap, lanes)
                ys[:, m, :, at_n] = (made * sgate[:, m]).astype(BF16)

        collect(0, g)

    def compute_b(g):
        select(1, g)
        dispatch(1, g)
        for m in range(2):
            @pl.loop(0, units // 128)
            def _(n):
                at_n = pl.ds(pl.multiple_of(n * 128, 128), 128)
                act[:, at_n] = dot_t(xs[:, m].reshape(4 * cap, width), wdn[m, at_n, :])

            grad = act[:, 0:units]
            pre = sav[m, 4 * g : 4 * g + 4].reshape(4 * cap, 2 * units)
            p, q = pre[:, 0:units].astype(F32), pre[:, units : 2 * units].astype(F32)
            sigma = 1.0 / (1.0 + jnp.exp(-p))
            hid[:, 0:units] = (grad * q * sigma * (1.0 + p * (1.0 - sigma))).astype(BF16)
            hid[:, units : 2 * units] = (grad * p * sigma).astype(BF16)

            @pl.loop(0, width // lanes)
            def _(n):
                at_n = pl.ds(pl.multiple_of(n * lanes, lanes), lanes)
                made = dot_t(hid[...], wgu[m, at_n, :]).reshape(4, cap, lanes)
                ys[:, m, :, at_n] = made.astype(BF16)

        collect(1, g)

    per_half = half // PIECE
    opps, msgs, rels = {}, {}, {}
    for d in range(2):
        for g in range(2):
            for i in range(per_half):
                r = pl.ds(i * PIECE, PIECE)
                r_high = pl.ds(half + i * PIECE, PIECE)
                opps[d, g, 0, i] = send(part.at[d, 4 * g + 2, r], opp.at[d, g, 0, r], up)
                opps[d, g, 1, i] = send(part.at[d, 4 * g + 2, r_high], opp.at[d, g, 1, r], down)
            for i in range(2 * per_half):
                r = pl.ds(i * PIECE, PIECE)
                msgs[d, g, 0, i] = send(part.at[d, 4 * g + 1, r], near.at[d, g, 0, r], up)
                msgs[d, g, 1, i] = send(part.at[d, 4 * g + 3, r], near.at[d, g, 1, r], down)
                rels[d, g, i] = send(part.at[d, 4 * g, r], rel.at[d, g, r], (nexts, prevs)[d][g])

    def combine_1(d, g):
        for i in range(per_half):
            opps[d, g, 0, i].start()
            opps[d, g, 1, i].start()
        for i in range(per_half):
            msgs[d, g, 0, per_half + i].start()
            msgs[d, g, 1, i].start()

    def combine_2(d, g):
        for i in range(per_half):
            r = pl.ds(i * PIECE, PIECE)
            r_high = pl.ds(half + i * PIECE, PIECE)
            opps[d, g, 0, i].wait_recv()
            part[d, 4 * g + 1, r] = (part[d, 4 * g + 1, r].astype(F32) + opp[d, g, 0, r].astype(F32)).astype(BF16)
            msgs[d, g, 0, i].start()
            opps[d, g, 1, i].wait_recv()
            part[d, 4 * g + 3, r_high] = (part[d, 4 * g + 3, r_high].astype(F32) + opp[d, g, 1, r].astype(F32)).astype(BF16)
            msgs[d, g, 1, per_half + i].start()

    def combine_3(d, g):
        for i in range(2 * per_half):
            r = pl.ds(i * PIECE, PIECE)
            msgs[d, g, 0, i].wait_recv()
            msgs[d, g, 1, i].wait_recv()
            total = part[d, 4 * g, r].astype(F32) + near[d, g, 0, r].astype(F32) + near[d, g, 1, r].astype(F32)
            if g == 0:
                total = total + tok[d, 0, r].astype(F32)
            part[d, 4 * g, r] = total.astype(BF16)
            rels[d, g, i].start()

    def finish(d):
        out = (out_f, out_b)[d]
        for i in range(2 * per_half):
            r = pl.ds(i * PIECE, PIECE)
            rels[d, 0, i].wait_recv()
            rels[d, 1, i].wait_recv()
            out[r, :] = (rel[d, 0, r].astype(F32) + rel[d, 1, r].astype(F32)).astype(BF16)

    tab_z.start()
    for copy in tab_y[0]:
        copy.start()
    own[0, 0, 0, 0].start()
    own[0, 0, 1, 1].start()
    own[0, 0, 0, 1].start()
    own[0, 0, 1, 0].start()
    over[0, 0].start()
    over[0, 1].start()
    for copy in twin_w + twin_s:
        copy.start()
    tab_y[0][0].wait_recv()
    tab_o[0].start()
    tab_z.wait_recv()
    for copy in tab_y[1]:
        copy.start()
    tab_y[1][0].wait_recv()
    tab_o[1].start()
    forward(0, 0)
    own[1, 0, 0, 0].start()
    own[1, 0, 1, 1].start()
    own[1, 0, 0, 1].start()
    own[1, 0, 1, 0].start()
    over[0, 0].wait_recv()
    over[1, 0].start()
    start_own(0, 1, 0)
    for copy in load_tok + load_w + load_s:
        copy.wait()
    for copy in twin_w + twin_s:
        copy.wait_recv()
    for copy in [tab_y[0][1], tab_y[1][1]] + tab_o:
        copy.wait_recv()
    complete(0, 0)
    compute_f(0)
    forward(1, 0)
    over[0, 1].wait_recv()
    over[1, 1].start()
    start_own(0, 1, 1)
    complete(1, 0)
    compute_b(0)
    forward(0, 1)
    over[1, 0].wait_recv()
    start_own(1, 1, 0)
    over[1, 1].wait_recv()
    start_own(1, 1, 1)
    complete(0, 1)
    compute_f(1)
    combine_1(0, 1)
    forward(1, 1)
    complete(1, 1)
    compute_b(1)
    combine_1(1, 1)
    combine_2(0, 1)
    combine_1(0, 0)
    combine_2(1, 1)
    combine_3(0, 1)
    combine_1(1, 0)
    combine_2(0, 0)
    combine_3(1, 1)
    combine_2(1, 0)
    combine_3(0, 0)
    combine_3(1, 0)
    finish(0)
    finish(1)
    for copy in remote:
        copy.wait_send()


def shards(
    fwd_tokens, fwd_experts, fwd_gates, gate_proj, up_proj, down_proj, bwd_grads, bwd_experts, bwd_gates, saved_pre
):
    rows, width = fwd_tokens.shape[1:]
    units = gate_proj.shape[3]
    cap = saved_pre.shape[3]
    table = jnp.concatenate(
        [fwd_experts[0].T.astype(F32), fwd_gates[0].T, bwd_experts[0].T.astype(F32), bwd_gates[0].T], axis=0
    )
    hbm = pl.BlockSpec(memory_space=pl.ANY)
    vmem = pl.BlockSpec(memory_space=pltpu.VMEM)
    copies = 128
    out = jax.ShapeDtypeStruct((rows, width), BF16)
    out_f, out_b = pl.pallas_call(
        body,
        out_shape=(out, out),
        in_specs=[vmem] + [hbm] * 6,
        out_specs=(vmem, vmem),
        scratch_shapes=[
            pltpu.VMEM((2, 8, rows, width), BF16),
            pltpu.VMEM((8, 32, rows), F32),
            pltpu.VMEM((2, width, 2 * units), BF16),
            pltpu.VMEM((2, units, width), BF16),
            pltpu.VMEM((2, 8, cap, 2 * units), BF16),
            pltpu.VMEM((4, 2, cap, width), BF16),
            pltpu.VMEM((4, 2, cap, width), BF16),
            pltpu.VMEM((4 * cap, 2 * units), F32),
            pltpu.VMEM((4 * cap, 2 * units), BF16),
            pltpu.VMEM((4, 2 * cap, rows), F32),
            pltpu.VMEM((4, rows, 2 * cap), BF16),
            pltpu.VMEM((4, 2, cap, 1), F32),
            pltpu.VMEM((16, rows), F32),
            pltpu.VMEM((2, 8, rows, width), BF16),
            pltpu.VMEM((2, 2, 2, rows // 2, width), BF16),
            pltpu.VMEM((2, 2, 2, rows, width), BF16),
            pltpu.VMEM((2, 2, rows, width), BF16),
            pltpu.SemaphoreType.DMA((copies,)),
            pltpu.SemaphoreType.DMA((copies,)),
            pltpu.SemaphoreType.DMA((16,)),
        ],
        compiler_params=pltpu.CompilerParams(
            collective_id=0, has_side_effects=True, vmem_limit_bytes=60 * 1024 * 1024
        ),
        cost_estimate=pl.CostEstimate(flops=16 * 10**9, bytes_accessed=12 * 10**6, transcendentals=10**6),
    )(
        table, fwd_tokens[0], bwd_grads[0], gate_proj[0, 0], up_proj[0, 0], down_proj[0, 0], saved_pre[0, :, 0]
    )
    return out_f[None], out_b[None]


def solution(mesh):
    rows = P("section", "expert", None)
    weights = P("section", "expert", None, None)
    placed = (rows, rows, rows, weights, weights, weights, rows, rows, rows, P("section", None, "expert", None, None))
    return jax.shard_map(shards, mesh=mesh, in_specs=placed, out_specs=(rows, rows), check_vma=False)
```

```python
import jax
import jax.numpy as jnp
from jax import lax
from jax.experimental import pallas as pl
from jax.experimental.pallas import tpu as pltpu
from jax.sharding import PartitionSpec as P

Y_SIZE, HALVES, CORES = 4, 2, 2
PIECES = tuple((16 * k, 16) for k in range(4))
MESH = pl.DeviceIdType.MESH
F32, BF16 = jnp.float32, jnp.bfloat16


def dot(a, b):
    return lax.dot_general(a, b, (((1,), (0,)), ((), ())), preferred_element_type=F32)


def dot_t(a, b):
    return lax.dot_general(a, b, (((1,), (1,)), ((), ())), preferred_element_type=F32)


def body(
    fe, fg, be, bg, xf, xb, wg, wu, wd, saved, rel_f, rel_b,
    tok, tab, wgu, wdn, sav, xs, ys, act, hid, sel, sel_t, sgate, chosen, part, opp, near,
    dma_send, dma_recv, dma_local,
):
    section, expert = lax.axis_index("section"), lax.axis_index("expert")
    sections = lax.axis_size("section")
    y, h, c = expert // (HALVES * CORES), (expert // CORES) % HALVES, expert % CORES
    rows, width = xf.shape
    units = wg.shape[1]
    cap = saved.shape[1]
    half = rows // 2

    def at(dy, dh=0, dc=0, ds=0):
        return (
            (section + ds + sections) % sections,
            (((y + dy + Y_SIZE) % Y_SIZE) * HALVES + (h + dh) % HALVES) * CORES + (c + dc) % CORES,
        )

    up, down, across, twin = at(1), at(-1), at(0, 1), at(0, 0, 1)
    nexts = (at(0, 0, 0, 1), at(0, 1, 0, 1))
    prevs = (at(0, 0, 0, -1), at(0, 1, 0, -1))

    count = [0, 0]
    remote = []

    def send(src, dst, device):
        i = count[0]
        count[0] += 1
        copy = pltpu.make_async_remote_copy(
            src_ref=src, dst_ref=dst, send_sem=dma_send.at[i], recv_sem=dma_recv.at[i],
            device_id=device, device_id_type=MESH,
        )
        remote.append(copy)
        return copy

    def local(src, dst):
        i = count[1]
        count[1] += 1
        return pltpu.make_async_copy(src, dst, dma_local.at[i])

    barrier = pltpu.get_barrier_semaphore()
    greeted = (up, down, across, twin) + nexts + prevs
    for device in greeted:
        pl.semaphore_signal(barrier, inc=1, device_id=device, device_id_type=MESH)

    inputs = (xf, xb)
    load_tok = [local(inputs[d], tok.at[d, 0]) for d in range(2)]
    load_w = [
        local(wg, wgu.at[0, :, pl.ds(0, units)]),
        local(wu, wgu.at[0, :, pl.ds(units, units)]),
        local(wd, wdn.at[0]),
    ]

    def block_of(j, core):
        hh, dy = j // Y_SIZE, j % Y_SIZE
        return (((y + dy) % Y_SIZE) * HALVES + (h + hh) % HALVES) * CORES + core

    load_s = [local(saved.at[block_of(j, c)], sav.at[0, j]) for j in range(8)]
    for copy in load_tok + load_w + load_s:
        copy.start()
    tab[0, 0:8, :] = fe[...].astype(F32)
    tab[0, 8:16, :] = fg[...]
    tab[0, 16:24, :] = be[...].astype(F32)
    tab[0, 24:32, :] = bg[...]
    pl.semaphore_wait(barrier, len(greeted))

    low, high = pl.ds(0, half), pl.ds(half, half)
    tab_z = send(tab.at[0], tab.at[4], across)
    tab_y = [(send(tab.at[4 * g], tab.at[4 * g + 3], up), send(tab.at[4 * g], tab.at[4 * g + 1], down)) for g in range(2)]
    tab_o = [send(tab.at[4 * g + 3], tab.at[4 * g + 2], up) for g in range(2)]

    def source(d, g, part_rows):
        return inputs[d].at[part_rows] if g == 0 else tok.at[d, 4, part_rows]

    own = {}
    fwd = {}
    over = {}
    for d in range(2):
        for i, r in enumerate((low, high)):
            over[d, i] = send(inputs[d].at[r], tok.at[d, 4, r], across)
        for g in range(2):
            for i, r in enumerate((low, high)):
                own[d, g, 0, i] = send(source(d, g, r), tok.at[d, 4 * g + 3, r], up)
                own[d, g, 1, i] = send(source(d, g, r), tok.at[d, 4 * g + 1, r], down)
            fwd[d, g, 0] = send(tok.at[d, 4 * g + 3, low], tok.at[d, 4 * g + 2, low], up)
            fwd[d, g, 1] = send(tok.at[d, 4 * g + 1, high], tok.at[d, 4 * g + 2, high], down)
    twin_w = [
        send(wg, wgu.at[1, :, pl.ds(0, units)], twin),
        send(wu, wgu.at[1, :, pl.ds(units, units)], twin),
        send(wd, wdn.at[1], twin),
    ]
    twin_s = [send(saved.at[block_of(j, 1 - c)], sav.at[1, j], twin) for j in range(8)]

    def start_own(d, g, i):
        own[d, g, 0, i].start()
        own[d, g, 1, i].start()

    def forward(d, g):
        own[d, g, 0, 0].wait_recv()
        fwd[d, g, 0].start()
        own[d, g, 1, 1].wait_recv()
        fwd[d, g, 1].start()

    def complete(d, g):
        own[d, g, 0, 1].wait_recv()
        own[d, g, 1, 0].wait_recv()
        fwd[d, g, 0].wait_recv()
        fwd[d, g, 1].wait_recv()

    experts = [(y * HALVES + h) * CORES + c, (y * HALVES + h) * CORES + (1 - c)]

    def select(d, g):
        for j in range(4):
            names = tab[4 * g + j, 16 * d : 16 * d + 8, :]
            gates = tab[4 * g + j, 16 * d + 8 : 16 * d + 16, :]
            for m in range(2):
                hit = names == experts[m].astype(F32)
                chosen[2 * j + m : 2 * j + m + 1, :] = jnp.sum(jnp.where(hit, 1.0, 0.0), axis=0, keepdims=True)
                chosen[8 + 2 * j + m : 9 + 2 * j + m, :] = jnp.sum(jnp.where(hit, gates, 0.0), axis=0, keepdims=True)
        earlier = lax.broadcasted_iota(jnp.int32, (rows, rows), 0) < lax.broadcasted_iota(jnp.int32, (rows, rows), 1)
        ahead = dot(chosen[0:8, :].astype(BF16), jnp.where(earlier, 1.0, 0.0).astype(BF16))
        place = lax.broadcasted_iota(jnp.int32, (cap, rows), 0).astype(F32)
        for j in range(4):
            for m in range(2):
                i = 2 * j + m
                taken = (place == ahead[i : i + 1, :]) & (chosen[i : i + 1, :] > 0.5)
                one = jnp.where(taken, 1.0, 0.0)
                sel[j, m * cap : (m + 1) * cap, :] = one
                sgate[j, m] = jnp.sum(one * chosen[8 + i : 9 + i, :], axis=1, keepdims=True)
            sel_t[j] = jnp.transpose(sel[j]).astype(BF16)

    def dispatch(d, g):
        for j in range(4):
            moved = dot(sel[j].astype(BF16), tok[d, 4 * g + j]).reshape(2, cap, width)
            if d == 1:
                moved = moved * sgate[j]
            xs[j] = moved.astype(BF16)

    def collect(d, g):
        for j in range(4):
            part[d, 4 * g + j] = dot(sel_t[j], ys[j].reshape(2 * cap, width)).astype(BF16)

    def compute_f(g):
        select(0, g)
        dispatch(0, g)
        for m in range(2):
            act[...] = dot(xs[:, m].reshape(4 * cap, width), wgu[m])
            gate = act[:, 0:units]
            hid[:, 0:units] = (gate / (1.0 + jnp.exp(-gate)) * act[:, units : 2 * units]).astype(BF16)
            made = dot(hid[:, 0:units], wdn[m]).reshape(4, cap, width)
            ys[:, m] = (made * sgate[:, m]).astype(BF16)
        collect(0, g)

    def compute_b(g):
        select(1, g)
        dispatch(1, g)
        for m in range(2):
            act[:, 0:units] = dot_t(xs[:, m].reshape(4 * cap, width), wdn[m])
            grad = act[:, 0:units]
            pre = sav[m, 4 * g : 4 * g + 4].reshape(4 * cap, 2 * units)
            p, q = pre[:, 0:units].astype(F32), pre[:, units : 2 * units].astype(F32)
            sigma = 1.0 / (1.0 + jnp.exp(-p))
            hid[:, 0:units] = (grad * q * sigma * (1.0 + p * (1.0 - sigma))).astype(BF16)
            hid[:, units : 2 * units] = (grad * p * sigma).astype(BF16)
            ys[:, m] = dot_t(hid[...], wgu[m]).reshape(4, cap, width).astype(BF16)
        collect(1, g)

    rels = (rel_f, rel_b)
    opps, msgs, outs = {}, {}, {}
    pieces = {}
    for d in range(2):
        for g in range(2):
            for k, (first, size) in enumerate(PIECES):
                lo, hi = pl.ds(first, size), pl.ds(half + first, size)
                pieces[g, k] = (lo, hi)
                opps[d, g, k, 0] = send(part.at[d, 4 * g + 2, lo], opp.at[d, g, 0, lo], up)
                opps[d, g, k, 1] = send(part.at[d, 4 * g + 2, hi], opp.at[d, g, 1, lo], down)
                for i, r in enumerate((lo, hi)):
                    msgs[d, g, k, 0, i] = send(part.at[d, 4 * g + 1, r], near.at[d, g, 0, r], up)
                    msgs[d, g, k, 1, i] = send(part.at[d, 4 * g + 3, r], near.at[d, g, 1, r], down)
                    outs[d, g, k, i] = send(part.at[d, 4 * g, r], rels[d].at[g, r], (nexts, prevs)[d][g])

    def begin(d, g, k):
        opps[d, g, k, 0].start()
        opps[d, g, k, 1].start()
        msgs[d, g, k, 0, 1].start()
        msgs[d, g, k, 1, 0].start()

    def add_on(d, g, k):
        lo, hi = pieces[g, k]
        for i, (r, j) in enumerate(((lo, 1), (hi, 3))):
            opps[d, g, k, i].wait_recv()
            part[d, 4 * g + j, r] = (part[d, 4 * g + j, r].astype(F32) + opp[d, g, i, lo].astype(F32)).astype(BF16)
            msgs[d, g, k, i, i].start()

    def relay(d, g, k):
        for i, r in enumerate(pieces[g, k]):
            msgs[d, g, k, 0, i].wait_recv()
            msgs[d, g, k, 1, i].wait_recv()
            total = part[d, 4 * g, r].astype(F32) + near[d, g, 0, r].astype(F32) + near[d, g, 1, r].astype(F32)
            if g == 0:
                total = total + tok[d, 0, r].astype(F32)
            part[d, 4 * g, r] = total.astype(BF16)
            outs[d, g, k, i].start()

    tab_z.start()
    for copy in tab_y[0]:
        copy.start()
    own[0, 0, 0, 0].start()
    own[0, 0, 1, 1].start()
    own[0, 0, 0, 1].start()
    own[0, 0, 1, 0].start()
    over[0, 0].start()
    over[0, 1].start()
    for copy in twin_w + twin_s:
        copy.start()
    tab_y[0][0].wait_recv()
    tab_o[0].start()
    tab_z.wait_recv()
    for copy in tab_y[1]:
        copy.start()
    tab_y[1][0].wait_recv()
    tab_o[1].start()
    forward(0, 0)
    own[1, 0, 0, 0].start()
    own[1, 0, 1, 1].start()
    own[1, 0, 0, 1].start()
    own[1, 0, 1, 0].start()
    over[0, 0].wait_recv()
    over[1, 0].start()
    start_own(0, 1, 0)
    for copy in load_tok + load_w + load_s:
        copy.wait()
    for copy in twin_w + twin_s:
        copy.wait_recv()
    for copy in [tab_y[0][1], tab_y[1][1]] + tab_o:
        copy.wait_recv()
    complete(0, 0)
    compute_f(0)
    forward(1, 0)
    over[0, 1].wait_recv()
    over[1, 1].start()
    start_own(0, 1, 1)
    complete(1, 0)
    compute_b(0)
    forward(0, 1)
    over[1, 0].wait_recv()
    start_own(1, 1, 0)
    over[1, 1].wait_recv()
    start_own(1, 1, 1)
    complete(0, 1)
    compute_f(1)
    jobs = [(0, 1, 0), (0, 1, 1), (1, 1, 0), (1, 1, 1), (1, 1, 2), (0, 1, 2), (1, 1, 3), (0, 1, 3)]
    jobs += [(d, 0, k) for k in range(len(PIECES)) for d in range(2)]
    for i in range(len(jobs) + 4):
        if i == 2:
            forward(1, 1)
            complete(1, 1)
            compute_b(1)
        if i < len(jobs):
            begin(*jobs[i])
        if 2 <= i < len(jobs) + 2:
            add_on(*jobs[i - 2])
        if i >= 4:
            relay(*jobs[i - 4])
    for copy in outs.values():
        copy.wait_recv()
    for copy in remote:
        copy.wait_send()


def shards(
    fwd_tokens, fwd_experts, fwd_gates, gate_proj, up_proj, down_proj, bwd_grads, bwd_experts, bwd_gates, saved_pre
):
    rows, width = fwd_tokens.shape[1:]
    units = gate_proj.shape[3]
    cap = saved_pre.shape[3]
    hbm = pl.BlockSpec(memory_space=pl.ANY)
    vmem = pl.BlockSpec(memory_space=pltpu.VMEM)
    copies = 256
    out = jax.ShapeDtypeStruct((2, rows, width), BF16)
    rel_f, rel_b = pl.pallas_call(
        body,
        out_shape=(out, out),
        in_specs=[vmem] * 4 + [hbm] * 6,
        out_specs=(hbm, hbm),
        scratch_shapes=[
            pltpu.VMEM((2, 8, rows, width), BF16),
            pltpu.VMEM((8, 32, rows), F32),
            pltpu.VMEM((2, width, 2 * units), BF16),
            pltpu.VMEM((2, units, width), BF16),
            pltpu.VMEM((2, 8, cap, 2 * units), BF16),
            pltpu.VMEM((4, 2, cap, width), BF16),
            pltpu.VMEM((4, 2, cap, width), BF16),
            pltpu.VMEM((4 * cap, 2 * units), F32),
            pltpu.VMEM((4 * cap, 2 * units), BF16),
            pltpu.VMEM((4, 2 * cap, rows), F32),
            pltpu.VMEM((4, rows, 2 * cap), BF16),
            pltpu.VMEM((4, 2, cap, 1), F32),
            pltpu.VMEM((16, rows), F32),
            pltpu.VMEM((2, 8, rows, width), BF16),
            pltpu.VMEM((2, 2, 2, rows // 2, width), BF16),
            pltpu.VMEM((2, 2, 2, rows, width), BF16),
            pltpu.SemaphoreType.DMA((copies,)),
            pltpu.SemaphoreType.DMA((copies,)),
            pltpu.SemaphoreType.DMA((16,)),
        ],
        compiler_params=pltpu.CompilerParams(
            collective_id=0, has_side_effects=True, vmem_limit_bytes=60 * 1024 * 1024
        ),
        cost_estimate=pl.CostEstimate(flops=16 * 10**9, bytes_accessed=12 * 10**6, transcendentals=10**6),
    )(
        fwd_experts[0].T, fwd_gates[0].T, bwd_experts[0].T, bwd_gates[0].T, fwd_tokens[0], bwd_grads[0],
        gate_proj[0, 0], up_proj[0, 0], down_proj[0, 0], saved_pre[0, :, 0],
    )
    return both(rel_f), both(rel_b)


def both(parts):
    return (parts[0:1].astype(F32) + parts[1:2].astype(F32)).astype(BF16)


def solution(mesh):
    rows = P("section", "expert", None)
    weights = P("section", "expert", None, None)
    placed = (rows, rows, rows, weights, weights, weights, rows, rows, rows, P("section", None, "expert", None, None))
    return jax.shard_map(shards, mesh=mesh, in_specs=placed, out_specs=(rows, rows), check_vma=False)
```

```python
import jax
import jax.numpy as jnp
from jax import lax
from jax.experimental import pallas as pl
from jax.experimental.pallas import tpu as pltpu
from jax.sharding import PartitionSpec as P

Y_SIZE, HALVES, CORES = 4, 2, 2
LIFT = 16
PIECES = tuple((16 * k, 16) for k in range(4))
MESH = pl.DeviceIdType.MESH
F32, BF16 = jnp.float32, jnp.bfloat16


def dot(a, b):
    return lax.dot_general(a, b, (((1,), (0,)), ((), ())), preferred_element_type=F32)


def dot_t(a, b):
    return lax.dot_general(a, b, (((1,), (1,)), ((), ())), preferred_element_type=F32)


def body(
    fe, fg, be, bg, xf, xb, wg, wu, wd, saved, rel_f, rel_b,
    tok, tab, wgu, wdn, sav, xs, ys, act, hid, sel, sel_t, sgate, chosen, part, opp, near, lift,
    dma_send, dma_recv, dma_local,
):
    section, expert = lax.axis_index("section"), lax.axis_index("expert")
    sections = lax.axis_size("section")
    y, h, c = expert // (HALVES * CORES), (expert // CORES) % HALVES, expert % CORES
    rows, width = xf.shape
    units = wg.shape[1]
    cap = saved.shape[1]
    half = rows // 2

    def at(dy, dh=0, dc=0, ds=0):
        return (
            (section + ds + sections) % sections,
            (((y + dy + Y_SIZE) % Y_SIZE) * HALVES + (h + dh) % HALVES) * CORES + (c + dc) % CORES,
        )

    up, down, across, twin = at(1), at(-1), at(0, 1), at(0, 0, 1)
    nexts = (at(0, 0, 0, 1), at(0, 1, 0, 1))
    prevs = (at(0, 0, 0, -1), at(0, 1, 0, -1))

    count = [0, 0]
    remote = []

    def send(src, dst, device):
        i = count[0]
        count[0] += 1
        copy = pltpu.make_async_remote_copy(
            src_ref=src, dst_ref=dst, send_sem=dma_send.at[i], recv_sem=dma_recv.at[i],
            device_id=device, device_id_type=MESH,
        )
        remote.append(copy)
        return copy

    def local(src, dst):
        i = count[1]
        count[1] += 1
        return pltpu.make_async_copy(src, dst, dma_local.at[i])

    barrier = pltpu.get_barrier_semaphore()
    greeted = (up, down, across, twin) + nexts + prevs
    for device in greeted:
        pl.semaphore_signal(barrier, inc=1, device_id=device, device_id_type=MESH)

    inputs = (xf, xb)
    load_tok = [local(inputs[d], tok.at[d, 0]) for d in range(2)]
    load_w = [
        local(wg, wgu.at[0, :, pl.ds(0, units)]),
        local(wu, wgu.at[0, :, pl.ds(units, units)]),
        local(wd, wdn.at[0]),
    ]

    def block_of(j, core):
        hh, dy = j // Y_SIZE, j % Y_SIZE
        return (((y + dy) % Y_SIZE) * HALVES + (h + hh) % HALVES) * CORES + core

    load_s = [local(saved.at[block_of(j, c)], sav.at[0, j]) for j in range(8)]
    for copy in load_tok + load_w + load_s:
        copy.start()
    tab[0, 0:8, :] = fe[...].astype(F32)
    tab[0, 8:16, :] = fg[...]
    tab[0, 16:24, :] = be[...].astype(F32)
    tab[0, 24:32, :] = bg[...]
    pl.semaphore_wait(barrier, len(greeted))

    low, high = pl.ds(0, half), pl.ds(half, half)
    rest_low, rest_high = pl.ds(LIFT, half - LIFT), pl.ds(half + LIFT, half - LIFT)
    lifted = (pl.ds(0, LIFT), pl.ds(half, LIFT))
    tab_z = send(tab.at[0], tab.at[4], across)
    tab_y = [(send(tab.at[4 * g], tab.at[4 * g + 3], up), send(tab.at[4 * g], tab.at[4 * g + 1], down)) for g in range(2)]
    tab_o = [send(tab.at[4 * g + 3], tab.at[4 * g + 2], up) for g in range(2)]

    def source(d, g, part_rows):
        return inputs[d].at[part_rows] if g == 0 else tok.at[d, 4, part_rows]

    own = {}
    fwd = {}
    over = {}
    for d in range(2):
        for i, r in enumerate((low, high)):
            over[d, i] = send(inputs[d].at[r], tok.at[d, 4, r], across)
        for g in range(2):
            halves = (low, high) if (d, g) != (1, 1) else (rest_low, rest_high)
            for i, r in enumerate(halves):
                own[d, g, 0, i] = send(source(d, g, r), tok.at[d, 4 * g + 3, r], up)
                own[d, g, 1, i] = send(source(d, g, r), tok.at[d, 4 * g + 1, r], down)
            fwd[d, g, 0] = send(tok.at[d, 4 * g + 3, halves[0]], tok.at[d, 4 * g + 2, halves[0]], up)
            fwd[d, g, 1] = send(tok.at[d, 4 * g + 1, halves[1]], tok.at[d, 4 * g + 2, halves[1]], down)
    cross = [send(tok.at[1, j, r], tok.at[1, 4 + j, r], across) for j in range(1, 4) for r in lifted]
    twin_w = [
        send(wg, wgu.at[1, :, pl.ds(0, units)], twin),
        send(wu, wgu.at[1, :, pl.ds(units, units)], twin),
        send(wd, wdn.at[1], twin),
    ]
    twin_s = [send(saved.at[block_of(j, 1 - c)], sav.at[1, j], twin) for j in range(8)]

    def start_own(d, g, i):
        own[d, g, 0, i].start()
        own[d, g, 1, i].start()

    def forward(d, g):
        own[d, g, 0, 0].wait_recv()
        fwd[d, g, 0].start()
        own[d, g, 1, 1].wait_recv()
        fwd[d, g, 1].start()

    def complete(d, g):
        own[d, g, 0, 1].wait_recv()
        own[d, g, 1, 0].wait_recv()
        fwd[d, g, 0].wait_recv()
        fwd[d, g, 1].wait_recv()

    experts = [(y * HALVES + h) * CORES + c, (y * HALVES + h) * CORES + (1 - c)]

    def select(d, g):
        for j in range(4):
            names = tab[4 * g + j, 16 * d : 16 * d + 8, :]
            gates = tab[4 * g + j, 16 * d + 8 : 16 * d + 16, :]
            for m in range(2):
                hit = names == experts[m].astype(F32)
                chosen[2 * j + m : 2 * j + m + 1, :] = jnp.sum(jnp.where(hit, 1.0, 0.0), axis=0, keepdims=True)
                chosen[8 + 2 * j + m : 9 + 2 * j + m, :] = jnp.sum(jnp.where(hit, gates, 0.0), axis=0, keepdims=True)
        earlier = lax.broadcasted_iota(jnp.int32, (rows, rows), 0) < lax.broadcasted_iota(jnp.int32, (rows, rows), 1)
        ahead = dot(chosen[0:8, :].astype(BF16), jnp.where(earlier, 1.0, 0.0).astype(BF16))
        place = lax.broadcasted_iota(jnp.int32, (cap, rows), 0).astype(F32)
        for j in range(4):
            for m in range(2):
                i = 2 * j + m
                taken = (place == ahead[i : i + 1, :]) & (chosen[i : i + 1, :] > 0.5)
                one = jnp.where(taken, 1.0, 0.0)
                sel[j, m * cap : (m + 1) * cap, :] = one
                sgate[j, m] = jnp.sum(one * chosen[8 + i : 9 + i, :], axis=1, keepdims=True)
            sel_t[j] = jnp.transpose(sel[j]).astype(BF16)

    def dispatch(d, g):
        for j in range(4):
            moved = dot(sel[j].astype(BF16), tok[d, 4 * g + j]).reshape(2, cap, width)
            if d == 1:
                moved = moved * sgate[j]
            xs[j] = moved.astype(BF16)

    def collect(d, g):
        for j in range(4):
            part[d, 4 * g + j] = dot(sel_t[j], ys[j].reshape(2 * cap, width)).astype(BF16)

    def compute_f(g):
        select(0, g)
        dispatch(0, g)
        for m in range(2):
            act[...] = dot(xs[:, m].reshape(4 * cap, width), wgu[m])
            gate = act[:, 0:units]
            hid[:, 0:units] = (gate / (1.0 + jnp.exp(-gate)) * act[:, units : 2 * units]).astype(BF16)
            made = dot(hid[:, 0:units], wdn[m]).reshape(4, cap, width)
            ys[:, m] = (made * sgate[:, m]).astype(BF16)
        collect(0, g)

    def compute_b(g):
        select(1, g)
        dispatch(1, g)
        for m in range(2):
            act[:, 0:units] = dot_t(xs[:, m].reshape(4 * cap, width), wdn[m])
            grad = act[:, 0:units]
            pre = sav[m, 4 * g : 4 * g + 4].reshape(4 * cap, 2 * units)
            p, q = pre[:, 0:units].astype(F32), pre[:, units : 2 * units].astype(F32)
            sigma = 1.0 / (1.0 + jnp.exp(-p))
            hid[:, 0:units] = (grad * q * sigma * (1.0 + p * (1.0 - sigma))).astype(BF16)
            hid[:, units : 2 * units] = (grad * p * sigma).astype(BF16)
            ys[:, m] = dot_t(hid[...], wgu[m]).reshape(4, cap, width).astype(BF16)
        collect(1, g)

    rels = (rel_f, rel_b)
    opps, msgs, outs = {}, {}, {}
    pieces = {}
    for d in range(2):
        for g in range(2):
            for k, (first, size) in enumerate(PIECES):
                lo, hi = pl.ds(first, size), pl.ds(half + first, size)
                pieces[g, k] = (lo, hi)
                for i, r in enumerate((lo, hi)):
                    outs[d, g, k, i] = send(part.at[d, 4 * g, r], rels[d].at[g, r], (nexts, prevs)[d][g])
                if (d, g, k) == (0, 1, 0):
                    continue
                opps[d, g, k, 0] = send(part.at[d, 4 * g + 2, lo], opp.at[d, g, 0, lo], up)
                opps[d, g, k, 1] = send(part.at[d, 4 * g + 2, hi], opp.at[d, g, 1, lo], down)
                for i, r in enumerate((lo, hi)):
                    msgs[d, g, k, 0, i] = send(part.at[d, 4 * g + 1, r], near.at[d, g, 0, r], up)
                    msgs[d, g, k, 1, i] = send(part.at[d, 4 * g + 3, r], near.at[d, g, 1, r], down)
    lifts = {(j, i): send(part.at[0, 4 + j, r], lift.at[j - 1, i], across) for j in range(1, 4) for i, r in enumerate(lifted)}

    def take_lifts():
        for (j, i), copy in lifts.items():
            copy.wait_recv()
            part[0, j, lifted[i]] = (part[0, j, lifted[i]].astype(F32) + lift[j - 1, i].astype(F32)).astype(BF16)

    def begin(d, g, k):
        opps[d, g, k, 0].start()
        opps[d, g, k, 1].start()
        msgs[d, g, k, 0, 1].start()
        msgs[d, g, k, 1, 0].start()

    def add_on(d, g, k):
        lo, hi = pieces[g, k]
        for i, (r, j) in enumerate(((lo, 1), (hi, 3))):
            opps[d, g, k, i].wait_recv()
            part[d, 4 * g + j, r] = (part[d, 4 * g + j, r].astype(F32) + opp[d, g, i, lo].astype(F32)).astype(BF16)
            msgs[d, g, k, i, i].start()

    def relay(d, g, k):
        for i, r in enumerate(pieces[g, k]):
            msgs[d, g, k, 0, i].wait_recv()
            msgs[d, g, k, 1, i].wait_recv()
            total = part[d, 4 * g, r].astype(F32) + near[d, g, 0, r].astype(F32) + near[d, g, 1, r].astype(F32)
            if g == 0:
                total = total + tok[d, 0, r].astype(F32)
            part[d, 4 * g, r] = total.astype(BF16)
            outs[d, g, k, i].start()

    tab_z.start()
    for copy in tab_y[0]:
        copy.start()
    own[0, 0, 0, 0].start()
    own[0, 0, 1, 1].start()
    own[0, 0, 0, 1].start()
    own[0, 0, 1, 0].start()
    over[0, 0].start()
    over[0, 1].start()
    for copy in twin_w + twin_s:
        copy.start()
    tab_y[0][0].wait_recv()
    tab_o[0].start()
    tab_z.wait_recv()
    for copy in tab_y[1]:
        copy.start()
    tab_y[1][0].wait_recv()
    tab_o[1].start()
    forward(0, 0)
    own[1, 0, 0, 0].start()
    own[1, 0, 1, 1].start()
    own[1, 0, 0, 1].start()
    own[1, 0, 1, 0].start()
    over[0, 0].wait_recv()
    over[1, 0].start()
    start_own(0, 1, 0)
    for copy in load_tok + load_w + load_s:
        copy.wait()
    for copy in twin_w + twin_s:
        copy.wait_recv()
    for copy in [tab_y[0][1], tab_y[1][1]] + tab_o:
        copy.wait_recv()
    complete(0, 0)
    compute_f(0)
    forward(1, 0)
    over[0, 1].wait_recv()
    over[1, 1].start()
    start_own(0, 1, 1)
    complete(1, 0)
    for copy in cross:
        copy.start()
    compute_b(0)
    forward(0, 1)
    over[1, 0].wait_recv()
    start_own(1, 1, 0)
    over[1, 1].wait_recv()
    start_own(1, 1, 1)
    complete(0, 1)
    compute_f(1)
    outs[0, 1, 0, 0].start()
    outs[0, 1, 0, 1].start()
    for copy in lifts.values():
        copy.start()
    begin(0, 1, 1)
    forward(1, 1)
    complete(1, 1)
    begin(0, 1, 2)
    for copy in cross:
        copy.wait_recv()
    add_on(0, 1, 1)
    compute_b(1)
    steps = {"B": begin, "A": add_on, "R": relay}
    for step in (
        "B110 B111 A012 B013",
        "A110 R011 A111 B112",
        "R110 R012 A013 B113",
        "A112 R111 B000 A113",
        "R013 R112 B100 A000",
        "R113 B001 A100",
        "B101 A001 R000",
        "B002 A101 R100",
        "B102 A002 R001",
        "B003 A102 R101",
        "B103 A003 R002",
        "A103 R102",
        "R003 R103",
    ):
        for name in step.split():
            d, g, k = (int(x) for x in name[1:])
            if name == "B000":
                take_lifts()
            steps[name[0]](d, g, k)
    for copy in outs.values():
        copy.wait_recv()
    for copy in remote:
        copy.wait_send()


def shards(
    fwd_tokens, fwd_experts, fwd_gates, gate_proj, up_proj, down_proj, bwd_grads, bwd_experts, bwd_gates, saved_pre
):
    rows, width = fwd_tokens.shape[1:]
    units = gate_proj.shape[3]
    cap = saved_pre.shape[3]
    hbm = pl.BlockSpec(memory_space=pl.ANY)
    vmem = pl.BlockSpec(memory_space=pltpu.VMEM)
    copies = 256
    out = jax.ShapeDtypeStruct((2, rows, width), BF16)
    rel_f, rel_b = pl.pallas_call(
        body,
        out_shape=(out, out),
        in_specs=[vmem] * 4 + [hbm] * 6,
        out_specs=(hbm, hbm),
        scratch_shapes=[
            pltpu.VMEM((2, 8, rows, width), BF16),
            pltpu.VMEM((8, 32, rows), F32),
            pltpu.VMEM((2, width, 2 * units), BF16),
            pltpu.VMEM((2, units, width), BF16),
            pltpu.VMEM((2, 8, cap, 2 * units), BF16),
            pltpu.VMEM((4, 2, cap, width), BF16),
            pltpu.VMEM((4, 2, cap, width), BF16),
            pltpu.VMEM((4 * cap, 2 * units), F32),
            pltpu.VMEM((4 * cap, 2 * units), BF16),
            pltpu.VMEM((4, 2 * cap, rows), F32),
            pltpu.VMEM((4, rows, 2 * cap), BF16),
            pltpu.VMEM((4, 2, cap, 1), F32),
            pltpu.VMEM((16, rows), F32),
            pltpu.VMEM((2, 8, rows, width), BF16),
            pltpu.VMEM((2, 2, 2, rows // 2, width), BF16),
            pltpu.VMEM((2, 2, 2, rows, width), BF16),
            pltpu.VMEM((3, 2, LIFT, width), BF16),
            pltpu.SemaphoreType.DMA((copies,)),
            pltpu.SemaphoreType.DMA((copies,)),
            pltpu.SemaphoreType.DMA((16,)),
        ],
        compiler_params=pltpu.CompilerParams(
            collective_id=0, has_side_effects=True, vmem_limit_bytes=60 * 1024 * 1024
        ),
        cost_estimate=pl.CostEstimate(flops=16 * 10**9, bytes_accessed=12 * 10**6, transcendentals=10**6),
    )(
        fwd_experts[0].T, fwd_gates[0].T, bwd_experts[0].T, bwd_gates[0].T, fwd_tokens[0], bwd_grads[0],
        gate_proj[0, 0], up_proj[0, 0], down_proj[0, 0], saved_pre[0, :, 0],
    )
    return both(rel_f), both(rel_b)


def both(parts):
    return (parts[0:1].astype(F32) + parts[1:2].astype(F32)).astype(BF16)


def solution(mesh):
    rows = P("section", "expert", None)
    weights = P("section", "expert", None, None)
    placed = (rows, rows, rows, weights, weights, weights, rows, rows, rows, P("section", None, "expert", None, None))
    return jax.shard_map(shards, mesh=mesh, in_specs=placed, out_specs=(rows, rows), check_vma=False)
```

```python
import jax
import jax.numpy as jnp
from jax import lax
from jax.experimental import pallas as pl
from jax.experimental.pallas import tpu as pltpu
from jax.sharding import PartitionSpec as P

Y_SIZE, HALVES, CORES = 4, 2, 2
LIFT = 16
PIECES = (
    tuple((16 * k, 16, 0, 2) for k in range(3)) + ((48, 16, 0, 1), (48, 16, 1, 1)),
    tuple((16 * k, 16, 0, 2) for k in range(4)),
)
MESH = pl.DeviceIdType.MESH
F32, BF16 = jnp.float32, jnp.bfloat16


def dot(a, b):
    return lax.dot_general(a, b, (((1,), (0,)), ((), ())), preferred_element_type=F32)


def dot_t(a, b):
    return lax.dot_general(a, b, (((1,), (1,)), ((), ())), preferred_element_type=F32)


def body(
    fe, fg, be, bg, xf, xb, wg, wu, wd, saved, rel_f, rel_b,
    tok, tab, wgu, wdn, sav, xs, ys, act, hid, sel, sel_t, sgate, chosen, part, opp, near, lift,
    dma_send, dma_recv, dma_local,
):
    section, expert = lax.axis_index("section"), lax.axis_index("expert")
    sections = lax.axis_size("section")
    y, h, c = expert // (HALVES * CORES), (expert // CORES) % HALVES, expert % CORES
    rows, width = xf.shape
    units = wg.shape[1]
    cap = saved.shape[1]
    half = rows // 2

    def at(dy, dh=0, dc=0, ds=0):
        return (
            (section + ds + sections) % sections,
            (((y + dy + Y_SIZE) % Y_SIZE) * HALVES + (h + dh) % HALVES) * CORES + (c + dc) % CORES,
        )

    up, down, across, twin = at(1), at(-1), at(0, 1), at(0, 0, 1)
    nexts = (at(0, 0, 0, 1), at(0, 1, 0, 1))
    prevs = (at(0, 0, 0, -1), at(0, 1, 0, -1))

    count = [0, 0]
    remote = []

    def send(src, dst, device):
        i = count[0]
        count[0] += 1
        copy = pltpu.make_async_remote_copy(
            src_ref=src, dst_ref=dst, send_sem=dma_send.at[i], recv_sem=dma_recv.at[i],
            device_id=device, device_id_type=MESH,
        )
        remote.append(copy)
        return copy

    def local(src, dst):
        i = count[1]
        count[1] += 1
        return pltpu.make_async_copy(src, dst, dma_local.at[i])

    barrier = pltpu.get_barrier_semaphore()
    greeted = (up, down, across, twin) + nexts + prevs
    for device in greeted:
        pl.semaphore_signal(barrier, inc=1, device_id=device, device_id_type=MESH)

    inputs = (xf, xb)
    load_tok = [local(inputs[d], tok.at[d, 0]) for d in range(2)]
    load_w = [
        local(wg, wgu.at[0, :, pl.ds(0, units)]),
        local(wu, wgu.at[0, :, pl.ds(units, units)]),
        local(wd, wdn.at[0]),
    ]

    def block_of(j, core):
        hh, dy = j // Y_SIZE, j % Y_SIZE
        return (((y + dy) % Y_SIZE) * HALVES + (h + hh) % HALVES) * CORES + core

    load_s = [local(saved.at[block_of(j, c)], sav.at[0, j]) for j in range(8)]
    for copy in load_tok + load_w + load_s:
        copy.start()
    tab[0, 0:8, :] = fe[...].astype(F32)
    tab[0, 8:16, :] = fg[...]
    tab[0, 16:24, :] = be[...].astype(F32)
    tab[0, 24:32, :] = bg[...]
    pl.semaphore_wait(barrier, len(greeted))

    low, high = pl.ds(0, half), pl.ds(half, half)
    rest_low, rest_high = pl.ds(LIFT, half - LIFT), pl.ds(half + LIFT, half - LIFT)
    lifted = (pl.ds(0, LIFT), pl.ds(half, LIFT))
    tab_z = send(tab.at[0], tab.at[4], across)
    tab_y = [(send(tab.at[4 * g], tab.at[4 * g + 3], up), send(tab.at[4 * g], tab.at[4 * g + 1], down)) for g in range(2)]
    tab_o = [send(tab.at[4 * g + 3], tab.at[4 * g + 2], up) for g in range(2)]

    def source(d, g, part_rows):
        return inputs[d].at[part_rows] if g == 0 else tok.at[d, 4, part_rows]

    own = {}
    fwd = {}
    over = {}
    for d in range(2):
        for i, r in enumerate((low, high)):
            over[d, i] = send(inputs[d].at[r], tok.at[d, 4, r], across)
        for g in range(2):
            halves = (low, high) if (d, g) != (1, 1) else (rest_low, rest_high)
            for i, r in enumerate(halves):
                own[d, g, 0, i] = send(source(d, g, r), tok.at[d, 4 * g + 3, r], up)
                own[d, g, 1, i] = send(source(d, g, r), tok.at[d, 4 * g + 1, r], down)
            fwd[d, g, 0] = send(tok.at[d, 4 * g + 3, halves[0]], tok.at[d, 4 * g + 2, halves[0]], up)
            fwd[d, g, 1] = send(tok.at[d, 4 * g + 1, halves[1]], tok.at[d, 4 * g + 2, halves[1]], down)
    cross = [send(tok.at[1, j, r], tok.at[1, 4 + j, r], across) for j in range(1, 4) for r in lifted]
    twin_w = [
        send(wg, wgu.at[1, :, pl.ds(0, units)], twin),
        send(wu, wgu.at[1, :, pl.ds(units, units)], twin),
        send(wd, wdn.at[1], twin),
    ]
    twin_s = [send(saved.at[block_of(j, 1 - c)], sav.at[1, j], twin) for j in range(8)]

    def start_own(d, g, i):
        own[d, g, 0, i].start()
        own[d, g, 1, i].start()

    def forward(d, g):
        own[d, g, 0, 0].wait_recv()
        fwd[d, g, 0].start()
        own[d, g, 1, 1].wait_recv()
        fwd[d, g, 1].start()

    def complete(d, g):
        own[d, g, 0, 1].wait_recv()
        own[d, g, 1, 0].wait_recv()
        fwd[d, g, 0].wait_recv()
        fwd[d, g, 1].wait_recv()

    experts = [(y * HALVES + h) * CORES + c, (y * HALVES + h) * CORES + (1 - c)]

    def select(d, g):
        for j in range(4):
            names = tab[4 * g + j, 16 * d : 16 * d + 8, :]
            gates = tab[4 * g + j, 16 * d + 8 : 16 * d + 16, :]
            for m in range(2):
                hit = names == experts[m].astype(F32)
                chosen[2 * j + m : 2 * j + m + 1, :] = jnp.sum(jnp.where(hit, 1.0, 0.0), axis=0, keepdims=True)
                chosen[8 + 2 * j + m : 9 + 2 * j + m, :] = jnp.sum(jnp.where(hit, gates, 0.0), axis=0, keepdims=True)
        earlier = lax.broadcasted_iota(jnp.int32, (rows, rows), 0) < lax.broadcasted_iota(jnp.int32, (rows, rows), 1)
        ahead = dot(chosen[0:8, :].astype(BF16), jnp.where(earlier, 1.0, 0.0).astype(BF16))
        place = lax.broadcasted_iota(jnp.int32, (cap, rows), 0).astype(F32)
        for j in range(4):
            for m in range(2):
                i = 2 * j + m
                taken = (place == ahead[i : i + 1, :]) & (chosen[i : i + 1, :] > 0.5)
                one = jnp.where(taken, 1.0, 0.0)
                sel[j, m * cap : (m + 1) * cap, :] = one
                sgate[j, m] = jnp.sum(one * chosen[8 + i : 9 + i, :], axis=1, keepdims=True)
            sel_t[j] = jnp.transpose(sel[j]).astype(BF16)

    def dispatch(d, g):
        for j in range(4):
            moved = dot(sel[j].astype(BF16), tok[d, 4 * g + j]).reshape(2, cap, width)
            if d == 1:
                moved = moved * sgate[j]
            xs[j] = moved.astype(BF16)

    def collect(d, g):
        for j in range(4):
            part[d, 4 * g + j] = dot(sel_t[j], ys[j].reshape(2 * cap, width)).astype(BF16)

    def compute_f(g):
        select(0, g)
        dispatch(0, g)
        for m in range(2):
            act[...] = dot(xs[:, m].reshape(4 * cap, width), wgu[m])
            gate = act[:, 0:units]
            hid[:, 0:units] = (gate / (1.0 + jnp.exp(-gate)) * act[:, units : 2 * units]).astype(BF16)
            made = dot(hid[:, 0:units], wdn[m]).reshape(4, cap, width)
            ys[:, m] = (made * sgate[:, m]).astype(BF16)
        collect(0, g)

    def compute_b(g):
        select(1, g)
        dispatch(1, g)
        for m in range(2):
            act[:, 0:units] = dot_t(xs[:, m].reshape(4 * cap, width), wdn[m])
            grad = act[:, 0:units]
            pre = sav[m, 4 * g : 4 * g + 4].reshape(4 * cap, 2 * units)
            p, q = pre[:, 0:units].astype(F32), pre[:, units : 2 * units].astype(F32)
            sigma = 1.0 / (1.0 + jnp.exp(-p))
            hid[:, 0:units] = (grad * q * sigma * (1.0 + p * (1.0 - sigma))).astype(BF16)
            hid[:, units : 2 * units] = (grad * p * sigma).astype(BF16)
            ys[:, m] = dot_t(hid[...], wgu[m]).reshape(4, cap, width).astype(BF16)
        collect(1, g)

    rels = (rel_f, rel_b)
    opps, msgs, outs = {}, {}, {}
    pieces = {}
    for d in range(2):
        for g in range(2):
            for k, (first, size, side, sides) in enumerate(PIECES[g]):
                lo, hi = pl.ds(first, size), pl.ds(half + first, size)
                cols = pl.ds(side * (width // 2), sides * (width // 2))
                pieces[g, k] = (lo, hi, cols)
                for i, r in enumerate((lo, hi)):
                    outs[d, g, k, i] = send(part.at[d, 4 * g, r, cols], rels[d].at[g, r, cols], (nexts, prevs)[d][g])
                if (d, g, k) == (0, 1, 0):
                    continue
                opps[d, g, k, 0] = send(part.at[d, 4 * g + 2, lo, cols], opp.at[d, g, 0, lo, cols], up)
                opps[d, g, k, 1] = send(part.at[d, 4 * g + 2, hi, cols], opp.at[d, g, 1, lo, cols], down)
                for i, r in enumerate((lo, hi)):
                    msgs[d, g, k, 0, i] = send(part.at[d, 4 * g + 1, r, cols], near.at[d, g, 0, r, cols], up)
                    msgs[d, g, k, 1, i] = send(part.at[d, 4 * g + 3, r, cols], near.at[d, g, 1, r, cols], down)
    lifts = {(j, i): send(part.at[0, 4 + j, r], lift.at[j - 1, i], across) for j in range(1, 4) for i, r in enumerate(lifted)}

    def take_lifts():
        for (j, i), copy in lifts.items():
            copy.wait_recv()
            part[0, j, lifted[i]] = (part[0, j, lifted[i]].astype(F32) + lift[j - 1, i].astype(F32)).astype(BF16)

    def begin(d, g, k):
        opps[d, g, k, 0].start()
        opps[d, g, k, 1].start()
        msgs[d, g, k, 0, 1].start()
        msgs[d, g, k, 1, 0].start()

    def add_on(d, g, k):
        lo, hi, cols = pieces[g, k]
        for i, (r, j) in enumerate(((lo, 1), (hi, 3))):
            opps[d, g, k, i].wait_recv()
            part[d, 4 * g + j, r, cols] = (
                part[d, 4 * g + j, r, cols].astype(F32) + opp[d, g, i, lo, cols].astype(F32)
            ).astype(BF16)
            msgs[d, g, k, i, i].start()

    def relay(d, g, k):
        cols = pieces[g, k][2]
        for i, r in enumerate(pieces[g, k][:2]):
            msgs[d, g, k, 0, i].wait_recv()
            msgs[d, g, k, 1, i].wait_recv()
            total = (
                part[d, 4 * g, r, cols].astype(F32)
                + near[d, g, 0, r, cols].astype(F32)
                + near[d, g, 1, r, cols].astype(F32)
            )
            if g == 0:
                total = total + tok[d, 0, r, cols].astype(F32)
            part[d, 4 * g, r, cols] = total.astype(BF16)
            outs[d, g, k, i].start()

    tab_z.start()
    for copy in tab_y[0]:
        copy.start()
    own[0, 0, 0, 0].start()
    own[0, 0, 1, 1].start()
    own[0, 0, 0, 1].start()
    own[0, 0, 1, 0].start()
    over[0, 0].start()
    over[0, 1].start()
    for copy in twin_w + twin_s:
        copy.start()
    tab_y[0][0].wait_recv()
    tab_o[0].start()
    tab_z.wait_recv()
    for copy in tab_y[1]:
        copy.start()
    tab_y[1][0].wait_recv()
    tab_o[1].start()
    forward(0, 0)
    own[1, 0, 0, 0].start()
    own[1, 0, 1, 1].start()
    own[1, 0, 0, 1].start()
    own[1, 0, 1, 0].start()
    over[0, 0].wait_recv()
    over[1, 0].start()
    start_own(0, 1, 0)
    for copy in load_tok + load_w + load_s:
        copy.wait()
    for copy in twin_w + twin_s:
        copy.wait_recv()
    for copy in [tab_y[0][1], tab_y[1][1]] + tab_o:
        copy.wait_recv()
    complete(0, 0)
    compute_f(0)
    forward(1, 0)
    over[0, 1].wait_recv()
    over[1, 1].start()
    start_own(0, 1, 1)
    complete(1, 0)
    for copy in cross:
        copy.start()
    compute_b(0)
    forward(0, 1)
    over[1, 0].wait_recv()
    start_own(1, 1, 0)
    over[1, 1].wait_recv()
    start_own(1, 1, 1)
    complete(0, 1)
    compute_f(1)
    outs[0, 1, 0, 0].start()
    outs[0, 1, 0, 1].start()
    for copy in lifts.values():
        copy.start()
    begin(0, 1, 1)
    forward(1, 1)
    complete(1, 1)
    begin(0, 1, 2)
    for copy in cross:
        copy.wait_recv()
    add_on(0, 1, 1)
    compute_b(1)
    steps = {"B": begin, "A": add_on, "R": relay}
    for step in (
        "B110 B111 A012 B013",
        "A110 R011 A111 B112",
        "R110 R012 A013 B113",
        "A112 R111 B000 A113",
        "R013 R112 B100 A000",
        "R113 B001 A100",
        "B101 A001 R000",
        "B002 A101 R100",
        "B102 A002 R001",
        "B003 A102 R101",
        "B103 A003 R002",
        "B004 A103 R102",
        "B104 A004 R003",
        "A104 R103",
        "R004 R104",
    ):
        for name in step.split():
            d, g, k = (int(x) for x in name[1:])
            if name == "B000":
                take_lifts()
            steps[name[0]](d, g, k)
    for copy in outs.values():
        copy.wait_recv()
    for copy in remote:
        copy.wait_send()


def shards(
    fwd_tokens, fwd_experts, fwd_gates, gate_proj, up_proj, down_proj, bwd_grads, bwd_experts, bwd_gates, saved_pre
):
    rows, width = fwd_tokens.shape[1:]
    units = gate_proj.shape[3]
    cap = saved_pre.shape[3]
    hbm = pl.BlockSpec(memory_space=pl.ANY)
    vmem = pl.BlockSpec(memory_space=pltpu.VMEM)
    copies = 256
    out = jax.ShapeDtypeStruct((2, rows, width), BF16)
    rel_f, rel_b = pl.pallas_call(
        body,
        out_shape=(out, out),
        in_specs=[vmem] * 4 + [hbm] * 6,
        out_specs=(hbm, hbm),
        scratch_shapes=[
            pltpu.VMEM((2, 8, rows, width), BF16),
            pltpu.VMEM((8, 32, rows), F32),
            pltpu.VMEM((2, width, 2 * units), BF16),
            pltpu.VMEM((2, units, width), BF16),
            pltpu.VMEM((2, 8, cap, 2 * units), BF16),
            pltpu.VMEM((4, 2, cap, width), BF16),
            pltpu.VMEM((4, 2, cap, width), BF16),
            pltpu.VMEM((4 * cap, 2 * units), F32),
            pltpu.VMEM((4 * cap, 2 * units), BF16),
            pltpu.VMEM((4, 2 * cap, rows), F32),
            pltpu.VMEM((4, rows, 2 * cap), BF16),
            pltpu.VMEM((4, 2, cap, 1), F32),
            pltpu.VMEM((16, rows), F32),
            pltpu.VMEM((2, 8, rows, width), BF16),
            pltpu.VMEM((2, 2, 2, rows // 2, width), BF16),
            pltpu.VMEM((2, 2, 2, rows, width), BF16),
            pltpu.VMEM((3, 2, LIFT, width), BF16),
            pltpu.SemaphoreType.DMA((copies,)),
            pltpu.SemaphoreType.DMA((copies,)),
            pltpu.SemaphoreType.DMA((16,)),
        ],
        compiler_params=pltpu.CompilerParams(
            collective_id=0, has_side_effects=True, vmem_limit_bytes=60 * 1024 * 1024
        ),
        cost_estimate=pl.CostEstimate(flops=16 * 10**9, bytes_accessed=12 * 10**6, transcendentals=10**6),
    )(
        fwd_experts[0].T, fwd_gates[0].T, bwd_experts[0].T, bwd_gates[0].T, fwd_tokens[0], bwd_grads[0],
        gate_proj[0, 0], up_proj[0, 0], down_proj[0, 0], saved_pre[0, :, 0],
    )
    return both(rel_f), both(rel_b)


def both(parts):
    return (parts[0:1].astype(F32) + parts[1:2].astype(F32)).astype(BF16)


def solution(mesh):
    rows = P("section", "expert", None)
    weights = P("section", "expert", None, None)
    placed = (rows, rows, rows, weights, weights, weights, rows, rows, rows, P("section", None, "expert", None, None))
    return jax.shard_map(shards, mesh=mesh, in_specs=placed, out_specs=(rows, rows), check_vma=False)
```
